128 devices in a mesh: gx: 16 (over z, x_lo, core), gy: 8 (over y, x_hi).
Axes of the slice: x: 4 (x_hi: 2, x_lo: 2; x = x_hi * 2 + x_lo), y: 4, z: 4, core: 2. Of those that a mesh axis runs over, the one named last changes fastest.
Arguments:
- density: float32 [512, 512, 512], P('gx', 'gy'), may hold values from -6 to 6
- radius_cells: int32 [2], replicated, may hold values from 1 to 32
Outputs:
- filtered: float32 [2, 512, 512, 512], P(None, 'gx', 'gy')
The draws below stay inside these ranges and needn't reach their ends.
All inputs are finite; a program needn't handle non-finite values.
Results may differ from the reference program's by a relative error of at most 0.0001.
Values sent between devices are 32-bit elements; how exact they have to be, the bound alone decides.
No kernel may reach another device: no remote copies, remote signals or barrier semaphores. Data moves between devices by JAX's collectives and lax.ppermute only.
A program may use at most 128 MiB of HBM per device.

```python
import math
import jax
import jax.numpy as jnp

N = 512
RADII = 2


def block_scale(rng, dims, cuts, low, largest):
    gain = 1.0
    for dim, blocks in cuts:
        heights = jax.random.uniform(jax.random.fold_in(jax.random.fold_in(rng, 6), dim), (blocks,), jnp.float32, low / len(cuts), largest / len(cuts))
        gain = gain * jnp.repeat(jnp.exp(heights), dims[dim] // blocks).reshape((-1,) + (1,) * (len(dims) - 1 - dim))
    return gain


def normal_values(stream_key, shape, deviation, most, split=(), kind=jnp.bfloat16):
    level = block_scale(stream_key, shape, split, -0.22, 0.18) if split else 1.0
    values = jax.random.normal(stream_key, shape, jnp.float32) * deviation * level
    return jnp.minimum(jnp.maximum(values, -most), most).astype(kind)


def setup_inputs(seed: int = 0) -> dict:
    keys = jax.random.split(jax.random.key(seed), 3)
    density = normal_values(keys[0], (N, N, N), 1.0, 6.0, ((0, 16), (1, 8)), jnp.float32)
    radius_cells = jax.random.randint(keys[1], (RADII,), 1, 33).astype(jnp.int32)
    return {"density": density, "radius_cells": radius_cells}


def window(u_value):
    is_small = u_value < 0.2
    safe_u = jnp.where(is_small, 1.0, u_value)
    closed_form = 3.0 * (jnp.sin(safe_u) - safe_u * jnp.cos(safe_u)) / (safe_u * safe_u * safe_u)
    series = 1.0 - u_value * u_value / 10.0 + u_value ** 4 / 280.0
    return jnp.where(is_small, series, closed_form)

def reference(density, radius_cells):
    spectrum = jnp.fft.fftn(density)
    indices = jnp.arange(N, dtype=jnp.int32)
    signed = jnp.where(indices > N // 2, indices - N, indices).astype(jnp.float32)
    squares = signed * signed
    k_squared = squares[:, None, None] + squares[None, :, None] + squares[None, None, :]
    k_length = 2.0 * math.pi / N * jnp.sqrt(k_squared)
    results = []
    for radius_index in range(RADII):
        weights = window(k_length * radius_cells[radius_index].astype(jnp.float32))
        results.append(jnp.real(jnp.fft.ifftn(spectrum * weights)).astype(jnp.float32))
    return jnp.stack(results)
```

```python
import math

import jax
import jax.numpy as jnp
import ml_dtypes
import numpy as np
from jax import lax
from jax.experimental import pallas as pl
from jax.experimental.pallas import tpu as pltpu
from jax.sharding import PartitionSpec as P

N = 512
HALF = 256
QUARTER = 128
GX = 16
GY = 8
AXES = ("gx", "gy")
F32 = jnp.float32
BF16 = jnp.bfloat16
VMEM_LIMIT = 56 * 1024 * 1024


def frequencies():
    m = np.arange(QUARTER)
    even = np.concatenate([2 * m, np.where(m == 0, 256, 2 * m)])
    odd = np.concatenate([2 * m + 1, 2 * m + 1])
    return even, odd


def basis():
    n = np.arange(HALF)
    tables = []
    for freq in frequencies():
        angle = 2.0 * np.pi / N * ((freq[:, None] * n[None, :]) % N)
        is_cos = (np.arange(HALF) < QUARTER) | (freq == 256)
        table = np.where(is_cos[:, None], np.cos(angle), np.sin(angle))
        weight = np.where((freq == 0) | (freq == 256), 1.0, 2.0)
        tables.append(table * np.sqrt(weight / N)[:, None])
    return np.stack(tables)


def two_parts(table):
    high = table.astype(ml_dtypes.bfloat16)
    low = (table - high.astype(np.float64)).astype(ml_dtypes.bfloat16)
    return high, low


def left_table(table):
    high, low = two_parts(table)
    return np.concatenate([high, high, low], axis=2)


def right_table(table):
    high, low = two_parts(table)
    return np.concatenate([high, high, low], axis=1)


def x_order():
    x = np.arange(HALF).reshape(8, 16, 2)
    return x.transpose(2, 0, 1).reshape(-1)


def split(value):
    high = value.astype(BF16)
    low = (value - high.astype(F32)).astype(BF16)
    return high, low


def head_kernel(d_ref, table_ref, o_ref):
    first = d_ref[:, :, :HALF].reshape(1024, HALF)
    second = d_ref[:, :, HALF:].reshape(1024, HALF)
    rows = o_ref.reshape(128 * 4 * 8, 128)
    for parity in range(2):
        high, low = split(first + second if parity == 0 else first - second)
        data = jnp.concatenate([high, low, high], axis=1)
        out = lax.dot_general(
            table_ref[parity], data, (((1,), (1,)), ((), ())), preferred_element_type=F32
        )
        for half in range(2):
            for x in range(8):
                rows[pl.ds((2 * parity + half) * 8 + x, 128, stride=32), :] = out[
                    half * 128 : (half + 1) * 128, x * 128 : (x + 1) * 128
                ]


def middle_kernel(r_ref, w_ref, yf_ref, xf_ref, xi_ref, yi_ref, o_ref, lhs_ref, rhs_ref):
    low_lanes = lax.broadcasted_iota(jnp.int32, (256, 128), 1) < 64

    def merge(a, b):
        return (
            jnp.where(low_lanes, a, pltpu.roll(b, 64, 1)),
            jnp.where(low_lanes, pltpu.roll(a, 64, 1), b),
        )

    def put_lhs(slot, rows, cols, value):
        high, low = split(value)
        lhs_ref[slot, pl.ds(rows, value.shape[0]), pl.ds(cols, value.shape[1])] = high
        lhs_ref[slot, pl.ds(rows, value.shape[0]), pl.ds(cols + HALF, value.shape[1])] = low

    def put_rhs(slot, cols, value):
        high, low = split(value)
        rhs_ref[slot, :HALF, pl.ds(cols, value.shape[1])] = high
        rhs_ref[slot, HALF:, pl.ds(cols, value.shape[1])] = low

    def times_right(slot, table):
        data = jnp.concatenate([lhs_ref[slot], lhs_ref[slot, :, :HALF]], axis=1)
        return jnp.dot(data, table, preferred_element_type=F32)

    def times_left(table, slot):
        data = jnp.concatenate([rhs_ref[slot], rhs_ref[slot, :HALF, :]], axis=0)
        return jnp.dot(table, data, preferred_element_type=F32)

    for pair in range(2):
        low_a = r_ref[:, 2 * pair, 0].reshape(256, 128)
        low_b = r_ref[:, 2 * pair + 1, 0].reshape(256, 128)
        high_a = r_ref[:, 2 * pair + 4, 0].reshape(256, 128)
        high_b = r_ref[:, 2 * pair + 5, 0].reshape(256, 128)
        for parity in range(2):
            a = low_a + high_a if parity == 0 else low_a - high_a
            b = low_b + high_b if parity == 0 else low_b - high_b
            even_x, odd_x = merge(a, b)
            put_lhs(parity, 0, pair * 128, even_x)
            put_lhs(parity, 256, pair * 128, odd_x)
    for parity in range(2):
        out = times_right(parity, yf_ref[parity]).reshape(2, 2, 128, HALF)
        put_rhs(0, parity * HALF, (out[:, 0] + out[:, 1]).reshape(HALF, HALF))
        put_rhs(1, parity * HALF, (out[:, 0] - out[:, 1]).reshape(HALF, HALF))
    for parity in range(2):
        spectrum = times_left(xf_ref[parity], parity)
        for field in range(2):
            weights = w_ref[0, field, parity * HALF : (parity + 1) * HALF, :]
            put_rhs(2 + 2 * field + parity, 0, spectrum * weights)
    for field in range(2):
        even = times_left(xi_ref[0], 2 + 2 * field)
        odd = times_left(xi_ref[1], 3 + 2 * field)
        for near in range(2):
            value = even + odd if near == 0 else even - odd
            for parity in range(2):
                for p in range(2):
                    put_lhs(
                        parity,
                        p * 256 + near * 128,
                        0,
                        value[p * 128 : (p + 1) * 128, parity * HALF : (parity + 1) * HALF],
                    )
        even = times_right(0, yi_ref[0])
        odd = times_right(1, yi_ref[1])
        for near in range(2):
            value = even + odd if near == 0 else even - odd
            for pair in range(2):
                cols = slice(pair * 128, (pair + 1) * 128)
                first, second = merge(value[:256, cols], value[256:, cols])
                o_ref[:, 4 * near + 2 * pair, 0, field] = first.reshape(16, 16, 128)
                o_ref[:, 4 * near + 2 * pair + 1, 0, field] = second.reshape(16, 16, 128)


def tail_kernel(b_ref, table_ref, o_ref):
    rows = b_ref.reshape(128 * 4 * 8, 128)
    for x in range(8):
        parts = []
        for parity in range(2):
            coefs = jnp.concatenate(
                [
                    rows[pl.ds((2 * parity + half) * 8 + x, 128, stride=32), :].T
                    for half in range(2)
                ],
                axis=1,
            )
            high, low = split(coefs)
            data = jnp.concatenate([high, low, high], axis=1)
            parts.append(jnp.dot(data, table_ref[parity], preferred_element_type=F32))
        o_ref[0, 2 * x : 2 * x + 2, :, :HALF] = (parts[0] + parts[1]).reshape(2, 64, HALF)
        o_ref[0, 2 * x : 2 * x + 2, :, HALF:] = (parts[0] - parts[1]).reshape(2, 64, HALF)


def window(u_value):
    is_small = u_value < 0.2
    safe_u = jnp.where(is_small, 1.0, u_value)
    closed_form = 3.0 * (jnp.sin(safe_u) - safe_u * jnp.cos(safe_u)) / (safe_u * safe_u * safe_u)
    series = 1.0 - u_value * u_value / 10.0 + u_value**4 / 280.0
    return jnp.where(is_small, series, closed_form)


def plane_windows(radius_cells):
    d = lax.axis_index(AXES)
    kz = jnp.stack([2 * d, jnp.where(d == 0, 256, 2 * d), 2 * d + 1]).astype(F32)
    freq = np.concatenate(frequencies()).astype(np.float32)
    squares = jnp.asarray(freq * freq)
    k_squared = (
        (kz * kz)[:, None, None] + squares[None, :, None] + squares[None, None, :]
    )
    k_length = 2.0 * math.pi / N * jnp.sqrt(k_squared)
    radius_values = radius_cells.astype(F32)
    return window(k_length[:, None] * radius_values[None, :, None, None])


def whole(shape):
    return pl.BlockSpec(shape, lambda *_: (0,) * len(shape))


def params(dims):
    return pltpu.CompilerParams(
        dimension_semantics=("arbitrary",) * dims, vmem_limit_bytes=VMEM_LIMIT
    )


def per_device(density, radius_cells):
    table = basis()
    back = table.transpose(0, 2, 1)
    x_table = table[:, :, x_order()]
    x_back = x_table.transpose(0, 2, 1)
    coefs = pl.pallas_call(
        head_kernel,
        grid=(2,),
        in_specs=[
            pl.BlockSpec((16, 64, N), lambda i: (i, 0, 0)),
            whole((2, HALF, 3 * HALF)),
        ],
        out_specs=pl.BlockSpec((128, 4, 8, 128), lambda i: (0, 0, i, 0)),
        out_shape=jax.ShapeDtypeStruct((128, 4, 16, 128), F32),
        compiler_params=params(1),
    )(density, jnp.asarray(left_table(table)))
    planes = lax.all_to_all(coefs, AXES, split_axis=0, concat_axis=0, tiled=True)
    weights = plane_windows(radius_cells)
    planes = planes.reshape(GX, GY, 4, 16, 128)
    filtered = pl.pallas_call(
        middle_kernel,
        grid=(4,),
        in_specs=[
            pl.BlockSpec((GX, GY, 1, 16, 128), lambda s: (0, 0, s, 0, 0)),
            pl.BlockSpec((1, 2, N, N), lambda s: (jnp.minimum(s, 2), 0, 0, 0)),
            whole((2, 3 * HALF, HALF)),
            whole((2, HALF, 3 * HALF)),
            whole((2, HALF, 3 * HALF)),
            whole((2, 3 * HALF, HALF)),
        ],
        out_specs=pl.BlockSpec((GX, GY, 1, 2, 16, 128), lambda s: (0, 0, s, 0, 0, 0)),
        out_shape=jax.ShapeDtypeStruct((GX, GY, 4, 2, 16, 128), F32),
        scratch_shapes=[
            pltpu.VMEM((2, N, N), BF16),
            pltpu.VMEM((6, N, N), BF16),
        ],
        compiler_params=params(1),
    )(
        planes,
        weights,
        jnp.asarray(right_table(back)),
        jnp.asarray(left_table(x_table)),
        jnp.asarray(left_table(x_back)),
        jnp.asarray(right_table(table)),
    )
    filtered = filtered.reshape(128, 4, 2, 16, 128)
    filtered = lax.all_to_all(filtered, AXES, split_axis=0, concat_axis=0, tiled=True)
    return pl.pallas_call(
        tail_kernel,
        grid=(2, 2),
        in_specs=[
            pl.BlockSpec((128, 4, 1, 8, 128), lambda f, i: (0, 0, f, i, 0)),
            whole((2, 3 * HALF, HALF)),
        ],
        out_specs=pl.BlockSpec((1, 16, 64, N), lambda f, i: (f, i, 0, 0)),
        out_shape=jax.ShapeDtypeStruct((2, 32, 64, N), F32),
        compiler_params=params(2),
    )(filtered, jnp.asarray(right_table(table)))


def solution(mesh):
    return jax.shard_map(
        per_device,
        mesh=mesh,
        in_specs=(P("gx", "gy", None), P()),
        out_specs=P(None, "gx", "gy", None),
        check_vma=False,
    )
```

```python
import math

import jax
import jax.numpy as jnp
import ml_dtypes
import numpy as np
from jax import lax
from jax.experimental import pallas as pl
from jax.experimental.pallas import tpu as pltpu
from jax.sharding import PartitionSpec as P

N = 512
HALF = 256
QUARTER = 128
GX = 16
GY = 8
AXES = ("gx", "gy")
F32 = jnp.float32
BF16 = jnp.bfloat16
MIB = 1024 * 1024


def frequencies():
    m = np.arange(QUARTER)
    even = np.concatenate([2 * m, np.where(m == 0, HALF, 2 * m)])
    odd = np.concatenate([2 * m + 1, 2 * m + 1])
    return even, odd


def basis():
    n = np.arange(HALF)
    tables = []
    for freq in frequencies():
        angle = 2.0 * np.pi / N * ((freq[:, None] * n[None, :]) % N)
        is_cos = (np.arange(HALF) < QUARTER) | (freq == HALF)
        table = np.where(is_cos[:, None], np.cos(angle), np.sin(angle))
        weight = np.where((freq == 0) | (freq == HALF), 1.0, 2.0)
        tables.append(table * np.sqrt(weight / N)[:, None])
    return np.stack(tables)


def two_parts(table):
    high = table.astype(ml_dtypes.bfloat16)
    low = (table - high.astype(np.float64)).astype(ml_dtypes.bfloat16)
    return jnp.asarray(np.concatenate([high, low], axis=2))


def split(value):
    high = value.astype(BF16)
    low = (value - high.astype(F32)).astype(BF16)
    return high, low


def join(high, low, axis):
    return jnp.concatenate([high, low, high], axis=axis)


def join_table(table, axis):
    high, low = table[:, :HALF], table[:, HALF:]
    return jnp.concatenate([high, high, low], axis=axis)


def head_kernel(d_ref, table_ref, o_ref):
    def rows(cols):
        return jnp.concatenate([d_ref[p, x, :, cols] for x in range(8) for p in range(2)], axis=0)

    first, second = rows(slice(0, HALF)), rows(slice(HALF, N))
    for parity in range(2):
        data = join(*split(first + second if parity == 0 else first - second), 1)
        out = lax.dot_general(
            join_table(table_ref[parity], 1),
            data,
            (((1,), (1,)), ((), ())),
            preferred_element_type=F32,
        )
        for half in range(2):
            part = out[half * 128 : (half + 1) * 128]
            chunks = jnp.stack([part[:, x * 128 : (x + 1) * 128] for x in range(8)])
            o_ref[:, 2 * parity + half] = jnp.swapaxes(chunks, 0, 1)


def middle_kernel(r_ref, w_ref, table_ref, back_ref, o_ref, lhs_ref, rhs_ref):
    low_lanes = lax.broadcasted_iota(jnp.int32, (16, 16, 128), 2) < 64

    def merge(a, b):
        return (
            jnp.where(low_lanes, a, pltpu.roll(b, 64, 2)),
            jnp.where(low_lanes, pltpu.roll(a, 64, 2), b),
        )

    def put_rhs(slot, value):
        high, low = split(value)
        rhs_ref[slot, :HALF, :] = high
        rhs_ref[slot, HALF:, :] = low

    def times_right(slot, table):
        data = lhs_ref[slot].reshape(N, N)
        data = join(data[:, :HALF], data[:, HALF:], 1)
        return jnp.dot(data, join_table(table, 0), preferred_element_type=F32)

    def times_left(table, slot):
        data = join(rhs_ref[slot, :HALF, :], rhs_ref[slot, HALF:, :], 0)
        return jnp.dot(join_table(table, 1), data, preferred_element_type=F32)

    def load(parity):
        for pair in range(2):
            low_a, low_b = r_ref[:, 2 * pair, 0], r_ref[:, 2 * pair + 1, 0]
            high_a, high_b = r_ref[:, 2 * pair + 4, 0], r_ref[:, 2 * pair + 5, 0]
            a = low_a + high_a if parity == 0 else low_a - high_a
            b = low_b + high_b if parity == 0 else low_b - high_b
            for p, value in enumerate(merge(a, b)):
                high, low = split(value)
                cols = slice(pair * 128, (pair + 1) * 128)
                lhs_ref[parity, :, p, :, cols] = high
                cols = slice(HALF + pair * 128, HALF + (pair + 1) * 128)
                lhs_ref[parity, :, p, :, cols] = low

    def forward_y(parity):
        return times_right(parity, back_ref[parity])

    def after_y(parity, out):
        put_rhs(2 * parity, out[:HALF] + out[HALF:])
        put_rhs(2 * parity + 1, out[:HALF] - out[HALF:])

    def forward_x(parity, x_parity):
        return times_left(table_ref[x_parity], 2 * parity + x_parity)

    def window_block(field, x_parity, parity):
        rows = slice(x_parity * 128, (x_parity + 1) * 128)
        if parity == 0:
            upper = w_ref[0, field, rows, :HALF]
        else:
            odd = w_ref[0, field, rows, HALF:]
            upper = jnp.concatenate([odd, odd], axis=1)
        if x_parity == 1:
            return jnp.concatenate([upper, upper], axis=0)
        last = w_ref[0, field, HALF:, :HALF]
        if parity == 1:
            last = w_ref[0, field, HALF:, HALF:]
            last = jnp.concatenate([last, last], axis=1)
        is_first = lax.broadcasted_iota(jnp.int32, (8, HALF), 0) == 0
        return jnp.concatenate([upper, jnp.where(is_first, last, upper[:8]), upper[8:]], axis=0)

    def after_x(parity, x_parity, out):
        for field in range(2):
            weights = window_block(field, x_parity, parity)
            put_rhs(4 + 4 * field + 2 * parity + x_parity, out * weights)

    def inverse_x(field, parity):
        slot = 4 + 4 * field + 2 * parity
        return times_left(back_ref[0], slot), times_left(back_ref[1], slot + 1)

    def after_inverse_x(field, parity, out):
        for near in range(2):
            value = out[0] + out[1] if near == 0 else out[0] - out[1]
            high, low = split(value)
            gx = slice(near * 8, (near + 1) * 8)
            lhs_ref[2 + 2 * field + parity, gx, :, :, :HALF] = high.reshape(8, 2, 16, HALF)
            lhs_ref[2 + 2 * field + parity, gx, :, :, HALF:] = low.reshape(8, 2, 16, HALF)

    def inverse_y(field, parity):
        return times_right(2 + 2 * field + parity, table_ref[parity])

    def finish(field, even, odd):
        for near in range(2):
            value = even + odd if near == 0 else even - odd
            value = value.reshape(16, 2, 16, HALF)
            for pair in range(2):
                cols = slice(pair * 128, (pair + 1) * 128)
                first, second = merge(value[:, 0, :, cols], value[:, 1, :, cols])
                o_ref[:, 4 * near + 2 * pair, 0, field] = first
                o_ref[:, 4 * near + 2 * pair + 1, 0, field] = second

    load(0)
    y0 = forward_y(0)
    load(1)
    y1 = forward_y(1)
    after_y(0, y0)
    x00 = forward_x(0, 0)
    x01 = forward_x(0, 1)
    after_y(1, y1)
    x10 = forward_x(1, 0)
    after_x(0, 0, x00)
    after_x(0, 1, x01)
    x11 = forward_x(1, 1)
    i00 = inverse_x(0, 0)
    after_x(1, 0, x10)
    after_x(1, 1, x11)
    i01 = inverse_x(0, 1)
    after_inverse_x(0, 0, i00)
    i10 = inverse_x(1, 0)
    after_inverse_x(0, 1, i01)
    f0 = inverse_y(0, 0)
    after_inverse_x(1, 0, i10)
    g0 = inverse_y(0, 1)
    i11 = inverse_x(1, 1)
    finish(0, f0, g0)
    f1 = inverse_y(1, 0)
    after_inverse_x(1, 1, i11)
    finish(1, f1, inverse_y(1, 1))


def tail_kernel(b_ref, table_ref, o_ref, lhs_ref):
    def load(parity):
        for half in range(2):
            chunks = jnp.swapaxes(b_ref[:, 2 * parity + half, 0], 0, 1)
            for x in range(8):
                rows = slice(x * 128, (x + 1) * 128)
                for part, value in enumerate(split(chunks[x])):
                    start = part * HALF + half * 128
                    lhs_ref[parity, rows, start : start + 128] = value.T

    def transform(parity):
        data = join(lhs_ref[parity, :, :HALF], lhs_ref[parity, :, HALF:], 1)
        return jnp.dot(data, join_table(table_ref[parity], 0), preferred_element_type=F32)

    def store(cols, value):
        value = value.reshape(8, 2, 64, HALF)
        for p in range(2):
            o_ref[0, p, :, :, cols] = value[:, p]

    load(0)
    even = transform(0)
    load(1)
    odd = transform(1)
    store(slice(0, HALF), even + odd)
    store(slice(HALF, N), even - odd)


def window(u_value):
    is_small = u_value < 0.2
    safe_u = jnp.where(is_small, 1.0, u_value)
    closed_form = 3.0 * (jnp.sin(safe_u) - safe_u * jnp.cos(safe_u)) / (safe_u * safe_u * safe_u)
    series = 1.0 - u_value * u_value / 10.0 + u_value**4 / 280.0
    return jnp.where(is_small, series, closed_form)


def plane_windows(radius_cells):
    d = lax.axis_index(AXES)
    kz = jnp.stack([2 * d, jnp.where(d == 0, HALF, 2 * d), 2 * d + 1]).astype(F32)
    even, odd = frequencies()
    rows = np.concatenate([even[:QUARTER], odd[:QUARTER], np.full(8, HALF)])
    cols = np.concatenate([even, odd[:QUARTER]])
    row_squares = jnp.asarray((rows * rows).astype(np.float32))
    col_squares = jnp.asarray((cols * cols).astype(np.float32))
    k_squared = (
        (kz * kz)[:, None, None] + row_squares[None, :, None] + col_squares[None, None, :]
    )
    k_length = 2.0 * math.pi / N * jnp.sqrt(k_squared)
    radius_values = radius_cells.astype(F32)
    return window(k_length[:, None] * radius_values[None, :, None, None])


def whole(shape):
    return pl.BlockSpec(shape, lambda *_: (0,) * len(shape))


TABLE = (2, HALF, N)


def z_forward(density, table):
    return pl.pallas_call(
        head_kernel,
        grid=(2,),
        in_specs=[pl.BlockSpec((2, 8, 64, N), lambda i: (0, i, 0, 0)), whole(TABLE)],
        out_specs=pl.BlockSpec((128, 4, 8, 128), lambda i: (0, 0, i, 0)),
        out_shape=jax.ShapeDtypeStruct((128, 4, 16, 128), F32),
        compiler_params=pltpu.CompilerParams(vmem_limit_bytes=56 * MIB),
    )(density.reshape(2, 16, 64, N), table)


def filter_planes(planes, weights, table, back):
    return pl.pallas_call(
        middle_kernel,
        grid=(4,),
        in_specs=[
            pl.BlockSpec((GX, GY, 1, 16, 128), lambda s: (0, 0, s, 0, 0)),
            pl.BlockSpec((1, 2, HALF + 8, HALF + QUARTER), lambda s: (jnp.minimum(s, 2), 0, 0, 0)),
            whole(TABLE),
            whole(TABLE),
        ],
        out_specs=pl.BlockSpec((GX, GY, 1, 2, 16, 128), lambda s: (0, 0, s, 0, 0, 0)),
        out_shape=jax.ShapeDtypeStruct((GX, GY, 4, 2, 16, 128), F32),
        scratch_shapes=[
            pltpu.VMEM((6, GX, 2, 16, N), BF16),
            pltpu.VMEM((12, N, HALF), BF16),
        ],
        compiler_params=pltpu.CompilerParams(vmem_limit_bytes=28 * MIB),
    )(planes, weights, table, back)


def z_inverse(filtered, table):
    out = pl.pallas_call(
        tail_kernel,
        grid=(2, 2),
        in_specs=[pl.BlockSpec((128, 4, 1, 8, 128), lambda f, i: (0, 0, f, i, 0)), whole(TABLE)],
        out_specs=pl.BlockSpec((1, 2, 8, 64, N), lambda f, i: (f, 0, i, 0, 0)),
        out_shape=jax.ShapeDtypeStruct((2, 2, 16, 64, N), F32),
        scratch_shapes=[pltpu.VMEM((2, 1024, N), BF16)],
        compiler_params=pltpu.CompilerParams(vmem_limit_bytes=28 * MIB),
    )(filtered, table)
    return out.reshape(2, 32, 64, N)


def exchange(pieces):
    return lax.all_to_all(pieces, AXES, split_axis=0, concat_axis=0, tiled=True)


def per_device(density, radius_cells):
    table = two_parts(basis())
    back = two_parts(basis().transpose(0, 2, 1))
    planes = exchange(z_forward(density, table))
    weights = plane_windows(radius_cells)
    filtered = filter_planes(planes.reshape(GX, GY, 4, 16, 128), weights, table, back)
    return z_inverse(exchange(filtered.reshape(128, 4, 2, 16, 128)), table)


def solution(mesh):
    return jax.shard_map(
        per_device,
        mesh=mesh,
        in_specs=(P("gx", "gy", None), P()),
        out_specs=P(None, "gx", "gy", None),
        check_vma=False,
    )
```

```python
import math

import jax
import jax.numpy as jnp
import ml_dtypes
import numpy as np
from jax import lax
from jax.experimental import pallas as pl
from jax.experimental.pallas import tpu as pltpu
from jax.sharding import PartitionSpec as P

N = 512
HALF = 256
QUARTER = 128
GX = 16
GY = 8
AXES = ("gx", "gy")
F32 = jnp.float32
BF16 = jnp.bfloat16
MIB = 1024 * 1024
CHUNK = 128


def frequencies():
    m = np.arange(QUARTER)
    even = np.concatenate([2 * m, np.where(m == 0, HALF, 2 * m)])
    odd = np.concatenate([2 * m + 1, 2 * m + 1])
    return even, odd


def basis():
    n = np.arange(HALF)
    tables = []
    for freq in frequencies():
        angle = 2.0 * np.pi / N * ((freq[:, None] * n[None, :]) % N)
        is_cos = (np.arange(HALF) < QUARTER) | (freq == HALF)
        table = np.where(is_cos[:, None], np.cos(angle), np.sin(angle))
        weight = np.where((freq == 0) | (freq == HALF), 1.0, 2.0)
        tables.append(table * np.sqrt(weight / N)[:, None])
    return np.stack(tables)


def two_parts(table):
    high = table.astype(ml_dtypes.bfloat16)
    low = (table - high.astype(np.float64)).astype(ml_dtypes.bfloat16)
    return jnp.asarray(np.concatenate([high, low], axis=2))


def split(value):
    high = value.astype(BF16)
    low = (value - high.astype(F32)).astype(BF16)
    return high, low


def join(high, low, axis):
    return jnp.concatenate([high, low, high], axis=axis)


def join_table(table, axis):
    high, low = table[:, :HALF], table[:, HALF:]
    return jnp.concatenate([high, high, low], axis=axis)


def head_kernel(d_ref, table_ref, o_ref):
    def rows(cols):
        return jnp.concatenate([d_ref[p, x, :, cols] for x in range(8) for p in range(2)], axis=0)

    first, second = rows(slice(0, HALF)), rows(slice(HALF, N))
    across = (((1,), (1,)), ((), ()))
    for parity in range(2):
        high, low = split(first + second if parity == 0 else first - second)
        table = jnp.concatenate([table_ref[parity, :, :HALF], table_ref[parity, :, HALF:]], axis=0)
        both = lax.dot_general(table, high, across, preferred_element_type=F32)
        out = both[:HALF] + both[HALF:]
        out += lax.dot_general(table[:HALF], low, across, preferred_element_type=F32)
        for half in range(2):
            part = out[half * 128 : (half + 1) * 128]
            chunks = jnp.stack([part[:, x * 128 : (x + 1) * 128] for x in range(8)])
            o_ref[:, 2 * parity + half] = jnp.swapaxes(chunks, 0, 1)


def middle_kernel(r_ref, w_ref, table_ref, back_ref, o_ref, *scratch):
    lhs_refs, rhs_refs = scratch[:6], scratch[6:]
    def merge(a, b):
        low_lanes = lax.broadcasted_iota(jnp.int32, a.shape, 2) < 64
        return (
            jnp.where(low_lanes, a, pltpu.roll(b, 64, 2)),
            jnp.where(low_lanes, pltpu.roll(a, 64, 2), b),
        )

    def put_rhs(slot, rows, value):
        high, low = split(value)
        rhs_refs[slot][rows, :] = high
        rhs_refs[slot][slice(rows.start + HALF, rows.stop + HALF), :] = low

    def times_right(slot, part, table):
        gx = slice(part * CHUNK // 32, (part + 1) * CHUNK // 32)
        data = lhs_refs[slot][gx].reshape(CHUNK, N)
        data = join(data[:, :HALF], data[:, HALF:], 1)
        return jnp.dot(data, join_table(table, 0), preferred_element_type=F32)

    def times_left(table, slot, part):
        rows = slice(part * CHUNK, (part + 1) * CHUNK)
        data = join(rhs_refs[slot][:HALF, :], rhs_refs[slot][HALF:, :], 0)
        return jnp.dot(join_table(table[rows], 1), data, preferred_element_type=F32)

    def load(parity, pair, half):
        gx = slice(half * 8, half * 8 + 8)
        low_a, low_b = r_ref[gx, 2 * pair, 0], r_ref[gx, 2 * pair + 1, 0]
        high_a, high_b = r_ref[gx, 2 * pair + 4, 0], r_ref[gx, 2 * pair + 5, 0]
        a = low_a + high_a if parity == 0 else low_a - high_a
        b = low_b + high_b if parity == 0 else low_b - high_b
        for p, value in enumerate(merge(a, b)):
            high, low = split(value)
            cols = slice(pair * 128, (pair + 1) * 128)
            lhs_refs[parity][gx, p, :, cols] = high
            cols = slice(HALF + pair * 128, HALF + (pair + 1) * 128)
            lhs_refs[parity][gx, p, :, cols] = low

    parts = HALF // CHUNK

    def forward_y(parity, part):
        table = back_ref[parity]
        return times_right(parity, part, table), times_right(parity, part + parts, table)

    def after_y(parity, part, out):
        rows = slice(part * CHUNK, (part + 1) * CHUNK)
        put_rhs(2 * parity, rows, out[0] + out[1])
        put_rhs(2 * parity + 1, rows, out[0] - out[1])

    def forward_x(parity, x_parity, part):
        return times_left(table_ref[x_parity], 2 * parity + x_parity, part)

    def window_block(field, x_parity, parity, part):
        begin = x_parity * 128 + part * CHUNK % 128
        rows = slice(begin, begin + CHUNK)

        def wide(rows):
            if parity == 0:
                return w_ref[0, field, rows, :HALF]
            odd = w_ref[0, field, rows, HALF:]
            return jnp.concatenate([odd, odd], axis=1)

        weights = wide(rows)
        if x_parity == 1 or part * CHUNK != 128:
            return weights
        is_first = lax.broadcasted_iota(jnp.int32, (8, HALF), 0) == 0
        last = wide(slice(HALF, HALF + 8))
        return jnp.concatenate([jnp.where(is_first, last, weights[:8]), weights[8:]], axis=0)

    def after_x(parity, x_parity, part, out):
        rows = slice(part * CHUNK, (part + 1) * CHUNK)
        for field in range(2):
            weights = window_block(field, x_parity, parity, part)
            put_rhs(4 + 4 * field + 2 * parity + x_parity, rows, out * weights)

    def inverse_x(field, parity, part):
        slot = 4 + 4 * field + 2 * parity
        return times_left(back_ref[0], slot, part), times_left(back_ref[1], slot + 1, part)

    def after_inverse_x(field, parity, part, out):
        count = CHUNK // 32
        for near in range(2):
            value = out[0] + out[1] if near == 0 else out[0] - out[1]
            high, low = split(value)
            gx = slice(near * 8 + part * count, near * 8 + (part + 1) * count)
            lhs_refs[2 + 2 * field + parity][gx, :, :, :HALF] = high.reshape(count, 2, 16, HALF)
            lhs_refs[2 + 2 * field + parity][gx, :, :, HALF:] = low.reshape(count, 2, 16, HALF)

    def inverse_y(field, part):
        return [times_right(2 + 2 * field + parity, part, table_ref[parity]) for parity in range(2)]

    def finish(field, part, out):
        count = CHUNK // 32
        gx = slice(part * count, (part + 1) * count)
        for near in range(2):
            value = out[0] + out[1] if near == 0 else out[0] - out[1]
            value = value.reshape(count, 2, 16, HALF)
            for pair in range(2):
                cols = slice(pair * 128, (pair + 1) * 128)
                first, second = merge(value[:, 0, :, cols], value[:, 1, :, cols])
                o_ref[gx, 4 * near + 2 * pair, 0, field] = first
                o_ref[gx, 4 * near + 2 * pair + 1, 0, field] = second

    steps = []

    def add(product, use, *where):
        steps.append((lambda: product(*where), lambda out: use(*where, out)))

    for parity in range(2):
        for part in range(parts):
            add(forward_y, after_y, parity, part)
    for parity in range(2):
        for x_parity in range(2):
            for part in range(parts):
                add(forward_x, after_x, parity, x_parity, part)
    for field in range(2):
        for parity in range(2):
            for part in range(parts):
                add(inverse_x, after_inverse_x, field, parity, part)
    for field in range(2):
        for part in range(2 * parts):
            add(inverse_y, finish, field, part)
    loads = [(parity, pair, half) for parity in range(2) for half in range(2) for pair in range(2)]
    for where in loads[:4]:
        load(*where)
    waiting = None
    for index, (product, use) in enumerate(steps):
        out = product()
        if index < parts:
            for where in loads[4 + index * 4 // parts : 4 + (index + 1) * 4 // parts]:
                load(*where)
        if waiting is not None:
            waiting()
        waiting = lambda use=use, out=out: use(out)
    waiting()


def tail_kernel(b_ref, table_ref, o_ref, *scratch):
    lhs_refs, even_ref = scratch[:2], scratch[2]

    def gather(parity, half):
        begin = pl.multiple_of(8 * pl.program_id(1), 8)
        block = b_ref[:, 2 * parity + half, pl.program_id(0), pl.ds(begin, 8), :]
        return jnp.swapaxes(block, 0, 1)

    def put(parity, half, x, value):
        for part, value in enumerate(split(value)):
            start = part * HALF + half * 128
            lhs_refs[parity][x * 128 : (x + 1) * 128, start : start + 128] = value.T

    def transform(parity, x):
        data = lhs_refs[parity][x * 128 : (x + 1) * 128, :]
        data = join(data[:, :HALF], data[:, HALF:], 1)
        return jnp.dot(data, join_table(table_ref[parity], 0), preferred_element_type=F32)

    def store(x, even, odd):
        o_ref[0, :, x, :, :HALF] = (even + odd).reshape(2, 64, HALF)
        o_ref[0, :, x, :, HALF:] = (even - odd).reshape(2, 64, HALF)

    for half in range(2):
        chunks = gather(0, half)
        for x in range(8):
            put(0, half, x, chunks[x])
    for x in range(8):
        even_ref[x] = transform(0, x)
        half = x // 4
        if x % 4 == 0:
            chunks = gather(1, half)
        for y in range(2 * (x % 4), 2 * (x % 4) + 2):
            put(1, half, y, chunks[y])
    waiting = None
    for x in range(8):
        odd = transform(1, x)
        if waiting is not None:
            store(*waiting)
        waiting = (x, even_ref[x], odd)
    store(*waiting)


def window(u_value):
    is_small = u_value < 0.2
    safe_u = jnp.where(is_small, 1.0, u_value)
    closed_form = 3.0 * (jnp.sin(safe_u) - safe_u * jnp.cos(safe_u)) / (safe_u * safe_u * safe_u)
    series = 1.0 - u_value * u_value / 10.0 + u_value**4 / 280.0
    return jnp.where(is_small, series, closed_form)


def plane_windows(radius_cells):
    d = lax.axis_index(AXES)
    kz = jnp.stack([2 * d, jnp.where(d == 0, HALF, 2 * d), 2 * d + 1]).astype(F32)
    even, odd = frequencies()
    rows = np.concatenate([even[:QUARTER], odd[:QUARTER], np.full(8, HALF)])
    cols = np.concatenate([even, odd[:QUARTER]])
    row_squares = jnp.asarray((rows * rows).astype(np.float32))
    col_squares = jnp.asarray((cols * cols).astype(np.float32))
    k_squared = (
        (kz * kz)[:, None, None] + row_squares[None, :, None] + col_squares[None, None, :]
    )
    k_length = 2.0 * math.pi / N * jnp.sqrt(k_squared)
    radius_values = radius_cells.astype(F32)
    return window(k_length[:, None] * radius_values[None, :, None, None])


def whole(shape):
    return pl.BlockSpec(shape, lambda *_: (0,) * len(shape))


TABLE = (2, HALF, N)


def z_forward(density, table):
    return pl.pallas_call(
        head_kernel,
        grid=(2,),
        in_specs=[pl.BlockSpec((2, 8, 64, N), lambda i: (0, i, 0, 0)), whole(TABLE)],
        out_specs=pl.BlockSpec((128, 4, 8, 128), lambda i: (0, 0, i, 0)),
        out_shape=jax.ShapeDtypeStruct((128, 4, 16, 128), F32),
        compiler_params=pltpu.CompilerParams(vmem_limit_bytes=56 * MIB),
    )(density.reshape(2, 16, 64, N), table)


def filter_planes(planes, weights, table, back):
    return pl.pallas_call(
        middle_kernel,
        grid=(4,),
        in_specs=[
            pl.BlockSpec((GX, GY, 1, 16, 128), lambda s: (0, 0, s, 0, 0)),
            pl.BlockSpec((1, 2, HALF + 8, HALF + QUARTER), lambda s: (jnp.minimum(s, 2), 0, 0, 0)),
            pl.BlockSpec(memory_space=pltpu.VMEM),
            pl.BlockSpec(memory_space=pltpu.VMEM),
        ],
        out_specs=pl.BlockSpec((GX, GY, 1, 2, 16, 128), lambda s: (0, 0, s, 0, 0, 0)),
        out_shape=jax.ShapeDtypeStruct((GX, GY, 4, 2, 16, 128), F32),
        scratch_shapes=[
            *[pltpu.VMEM((GX, 2, 16, N), BF16) for _ in range(6)],
            *[pltpu.VMEM((N, HALF), BF16) for _ in range(12)],
        ],
        compiler_params=pltpu.CompilerParams(vmem_limit_bytes=28 * MIB),
    )(planes, weights, table, back)


def z_inverse(filtered, table):
    out = pl.pallas_call(
        tail_kernel,
        grid=(2, 2),
        in_specs=[pl.BlockSpec(memory_space=pltpu.VMEM), pl.BlockSpec(memory_space=pltpu.VMEM)],
        out_specs=pl.BlockSpec((1, 2, 8, 64, N), lambda f, i: (f, 0, i, 0, 0)),
        out_shape=jax.ShapeDtypeStruct((2, 2, 16, 64, N), F32),
        scratch_shapes=[
            *[pltpu.VMEM((1024, N), BF16) for _ in range(2)],
            pltpu.VMEM((8, 128, HALF), F32),
        ],
        compiler_params=pltpu.CompilerParams(vmem_limit_bytes=28 * MIB),
    )(filtered, table)
    return out.reshape(2, 32, 64, N)


def exchange(pieces):
    return lax.all_to_all(pieces, AXES, split_axis=0, concat_axis=0, tiled=True)


def per_device(density, radius_cells):
    table = two_parts(basis())
    back = two_parts(basis().transpose(0, 2, 1))
    planes = exchange(z_forward(density, table))
    weights = plane_windows(radius_cells)
    filtered = filter_planes(planes.reshape(GX, GY, 4, 16, 128), weights, table, back)
    return z_inverse(exchange(filtered.reshape(128, 4, 2, 16, 128)), table)


def solution(mesh):
    return jax.shard_map(
        per_device,
        mesh=mesh,
        in_specs=(P("gx", "gy", None), P()),
        out_specs=P(None, "gx", "gy", None),
        check_vma=False,
    )
```

```python
import math

import jax
import jax.numpy as jnp
import ml_dtypes
import numpy as np
from jax import lax
from jax.experimental import pallas as pl
from jax.experimental.pallas import tpu as pltpu
from jax.sharding import PartitionSpec as P

N = 512
HALF = 256
QUARTER = 128
GX = 16
GY = 8
AXES = ("gx", "gy")
F32 = jnp.float32
BF16 = jnp.bfloat16
MIB = 1024 * 1024
CHUNK = 128


def frequencies():
    m = np.arange(QUARTER)
    even = np.concatenate([2 * m, np.where(m == 0, HALF, 2 * m)])
    odd = np.concatenate([2 * m + 1, 2 * m + 1])
    return even, odd


def basis():
    n = np.arange(HALF)
    tables = []
    for freq in frequencies():
        angle = 2.0 * np.pi / N * ((freq[:, None] * n[None, :]) % N)
        is_cos = (np.arange(HALF) < QUARTER) | (freq == HALF)
        table = np.where(is_cos[:, None], np.cos(angle), np.sin(angle))
        weight = np.where((freq == 0) | (freq == HALF), 1.0, 2.0)
        tables.append(table * np.sqrt(weight / N)[:, None])
    return np.stack(tables)


def two_parts(table):
    high = table.astype(ml_dtypes.bfloat16)
    low = (table - high.astype(np.float64)).astype(ml_dtypes.bfloat16)
    return jnp.asarray(np.concatenate([high, low], axis=2))


def split(value):
    high = value.astype(BF16)
    low = (value - high.astype(F32)).astype(BF16)
    return high, low


def join(high, low, axis):
    return jnp.concatenate([high, low, high], axis=axis)


def join_table(table, axis):
    high, low = table[:, :HALF], table[:, HALF:]
    return jnp.concatenate([high, high, low], axis=axis)


def head_kernel(d_ref, table_ref, o_ref):
    def rows(cols):
        return jnp.concatenate([d_ref[p, x, :, cols] for x in range(8) for p in range(2)], axis=0)

    first, second = rows(slice(0, HALF)), rows(slice(HALF, N))
    across = (((1,), (1,)), ((), ()))
    for parity in range(2):
        high, low = split(first + second if parity == 0 else first - second)
        table = jnp.concatenate([table_ref[parity, :, :HALF], table_ref[parity, :, HALF:]], axis=0)
        both = lax.dot_general(table, high, across, preferred_element_type=F32)
        out = both[:HALF] + both[HALF:]
        out += lax.dot_general(table[:HALF], low, across, preferred_element_type=F32)
        for half in range(2):
            part = out[half * 128 : (half + 1) * 128]
            chunks = jnp.stack([part[:, x * 128 : (x + 1) * 128] for x in range(8)])
            o_ref[:, 2 * parity + half] = jnp.swapaxes(chunks, 0, 1)


def middle_kernel(r_ref, w_ref, table_ref, back_ref, o_ref, *scratch):
    lhs_refs, rhs_refs = scratch[:6], scratch[6:]
    def merge(a, b):
        low_lanes = lax.broadcasted_iota(jnp.int32, a.shape, 2) < 64
        return (
            jnp.where(low_lanes, a, pltpu.roll(b, 64, 2)),
            jnp.where(low_lanes, pltpu.roll(a, 64, 2), b),
        )

    def put_rhs(slot, rows, value):
        high, low = split(value)
        rhs_refs[slot][rows, :] = high
        rhs_refs[slot][slice(rows.start + HALF, rows.stop + HALF), :] = low

    def times_right(slot, part, table):
        gx = slice(part * CHUNK // 32, (part + 1) * CHUNK // 32)
        data = lhs_refs[slot][gx].reshape(CHUNK, N)
        data = join(data[:, :HALF], data[:, HALF:], 1)
        return jnp.dot(data, join_table(table, 0), preferred_element_type=F32)

    def times_left(table, slot, part):
        rows = slice(part * CHUNK, (part + 1) * CHUNK)
        data = join(rhs_refs[slot][:HALF, :], rhs_refs[slot][HALF:, :], 0)
        return jnp.dot(join_table(table[rows], 1), data, preferred_element_type=F32)

    def load(parity, pair, half):
        gx = slice(half * 8, half * 8 + 8)
        low_a, low_b = r_ref[gx, 2 * pair, 0], r_ref[gx, 2 * pair + 1, 0]
        high_a, high_b = r_ref[gx, 2 * pair + 4, 0], r_ref[gx, 2 * pair + 5, 0]
        a = low_a + high_a if parity == 0 else low_a - high_a
        b = low_b + high_b if parity == 0 else low_b - high_b
        for p, value in enumerate(merge(a, b)):
            high, low = split(value)
            cols = slice(pair * 128, (pair + 1) * 128)
            lhs_refs[parity][gx, p, :, cols] = high
            cols = slice(HALF + pair * 128, HALF + (pair + 1) * 128)
            lhs_refs[parity][gx, p, :, cols] = low

    parts = HALF // CHUNK

    def forward_y(parity, part):
        table = back_ref[parity]
        return times_right(parity, part, table), times_right(parity, part + parts, table)

    def after_y(parity, part, out):
        rows = slice(part * CHUNK, (part + 1) * CHUNK)
        put_rhs(2 * parity, rows, out[0] + out[1])
        put_rhs(2 * parity + 1, rows, out[0] - out[1])

    def forward_x(parity, x_parity, part):
        return times_left(table_ref[x_parity], 2 * parity + x_parity, part)

    def window_block(field, x_parity, parity, part):
        begin = x_parity * 128 + part * CHUNK % 128
        rows = slice(begin, begin + CHUNK)

        def wide(rows):
            if parity == 0:
                return w_ref[0, field, rows, :HALF]
            odd = w_ref[0, field, rows, HALF:]
            return jnp.concatenate([odd, odd], axis=1)

        weights = wide(rows)
        if x_parity == 1 or part * CHUNK != 128:
            return weights
        is_first = lax.broadcasted_iota(jnp.int32, (8, HALF), 0) == 0
        last = wide(slice(HALF, HALF + 8))
        return jnp.concatenate([jnp.where(is_first, last, weights[:8]), weights[8:]], axis=0)

    def after_x(parity, x_parity, part, out):
        rows = slice(part * CHUNK, (part + 1) * CHUNK)
        for field in range(2):
            weights = window_block(field, x_parity, parity, part)
            put_rhs(4 + 4 * field + 2 * parity + x_parity, rows, out * weights)

    def inverse_x(field, parity, part):
        slot = 4 + 4 * field + 2 * parity
        return times_left(back_ref[0], slot, part), times_left(back_ref[1], slot + 1, part)

    def after_inverse_x(field, parity, part, out):
        count = CHUNK // 32
        for near in range(2):
            value = out[0] + out[1] if near == 0 else out[0] - out[1]
            high, low = split(value)
            gx = slice(near * 8 + part * count, near * 8 + (part + 1) * count)
            lhs_refs[2 + 2 * field + parity][gx, :, :, :HALF] = high.reshape(count, 2, 16, HALF)
            lhs_refs[2 + 2 * field + parity][gx, :, :, HALF:] = low.reshape(count, 2, 16, HALF)

    def inverse_y(field, part):
        return [times_right(2 + 2 * field + parity, part, table_ref[parity]) for parity in range(2)]

    def finish(field, part, out):
        count = CHUNK // 32
        gx = slice(part * count, (part + 1) * count)
        for near in range(2):
            value = out[0] + out[1] if near == 0 else out[0] - out[1]
            value = value.reshape(count, 2, 16, HALF)
            for pair in range(2):
                cols = slice(pair * 128, (pair + 1) * 128)
                first, second = merge(value[:, 0, :, cols], value[:, 1, :, cols])
                o_ref[gx, 4 * near + 2 * pair, 0, field] = first
                o_ref[gx, 4 * near + 2 * pair + 1, 0, field] = second

    steps = []

    def add(product, use, *where):
        steps.append((lambda: product(*where), lambda out: use(*where, out)))

    for parity in range(2):
        for part in range(parts):
            add(forward_y, after_y, parity, part)
    for parity in range(2):
        for x_parity in range(2):
            for part in range(parts):
                add(forward_x, after_x, parity, x_parity, part)
    for field in range(2):
        for parity in range(2):
            for part in range(parts):
                add(inverse_x, after_inverse_x, field, parity, part)
    for field in range(2):
        for part in range(2 * parts):
            add(inverse_y, finish, field, part)
    loads = [(parity, pair, half) for parity in range(2) for half in range(2) for pair in range(2)]
    for where in loads[:4]:
        load(*where)
    waiting = None
    for index, (product, use) in enumerate(steps):
        out = product()
        if index < parts:
            for where in loads[4 + index * 4 // parts : 4 + (index + 1) * 4 // parts]:
                load(*where)
        if waiting is not None:
            waiting()
        waiting = lambda use=use, out=out: use(out)
    waiting()


def tail_kernel(b_ref, table_ref, o_ref, stage_ref, done, *scratch):
    lhs_refs, even_refs = scratch[:4], scratch[4:]

    def gather(block, parity, half):
        rows = slice(8 * (block % 2), 8 * (block % 2) + 8)
        return jnp.swapaxes(b_ref[:, 2 * parity + half, block // 2, rows, :], 0, 1)

    def put(block, parity, half, x, value):
        for part, value in enumerate(split(value)):
            start = part * HALF + half * 128
            rows = slice(x * 128, (x + 1) * 128)
            lhs_refs[2 * (block % 2) + parity][rows, start : start + 128] = value.T

    def transform(block, parity, x):
        data = lhs_refs[2 * (block % 2) + parity][x * 128 : (x + 1) * 128, :]
        data = join(data[:, :HALF], data[:, HALF:], 1)
        return jnp.dot(data, join_table(table_ref[parity], 0), preferred_element_type=F32)

    def send(block, x):
        return pltpu.make_async_copy(
            stage_ref.at[block, x],
            o_ref.at[block // 2, :, 8 * (block % 2) + x],
            done.at[8 * block + x],
        )

    def store(block, x, even, odd):
        stage_ref[block, x, :, :, :HALF] = (even + odd).reshape(2, 64, HALF)
        stage_ref[block, x, :, :, HALF:] = (even - odd).reshape(2, 64, HALF)
        send(block, x).start()

    waiting = None
    for block in range(4):
        for half in range(2):
            chunks = gather(block, 0, half)
            for x in range(8):
                put(block, 0, half, x, chunks[x])
        for parity in range(2):
            for x in range(8):
                out = transform(block, parity, x)
                following = (block, 1)
                if parity == 0:
                    half = x // 4
                    if x % 4 == 0:
                        chunks = gather(*following, half)
                    for y in range(2 * (x % 4), 2 * (x % 4) + 2):
                        put(*following, half, y, chunks[y])
                if waiting is not None:
                    store(*waiting)
                    waiting = None
                if parity == 0:
                    even_refs[block % 2][x] = out
                else:
                    waiting = (block, x, even_refs[block % 2][x], out)
    store(*waiting)
    for block in range(4):
        for x in range(8):
            send(block, x).wait()


def window(u_value):
    is_small = u_value < 0.2
    safe_u = jnp.where(is_small, 1.0, u_value)
    closed_form = 3.0 * (jnp.sin(safe_u) - safe_u * jnp.cos(safe_u)) / (safe_u * safe_u * safe_u)
    series = 1.0 - u_value * u_value / 10.0 + u_value**4 / 280.0
    return jnp.where(is_small, series, closed_form)


def plane_windows(radius_cells):
    d = lax.axis_index(AXES)
    kz = jnp.stack([2 * d, jnp.where(d == 0, HALF, 2 * d), 2 * d + 1]).astype(F32)
    even, odd = frequencies()
    rows = np.concatenate([even[:QUARTER], odd[:QUARTER], np.full(8, HALF)])
    cols = np.concatenate([even, odd[:QUARTER]])
    row_squares = jnp.asarray((rows * rows).astype(np.float32))
    col_squares = jnp.asarray((cols * cols).astype(np.float32))
    k_squared = (
        (kz * kz)[:, None, None] + row_squares[None, :, None] + col_squares[None, None, :]
    )
    k_length = 2.0 * math.pi / N * jnp.sqrt(k_squared)
    radius_values = radius_cells.astype(F32)
    return window(k_length[:, None] * radius_values[None, :, None, None])


def whole(shape):
    return pl.BlockSpec(shape, lambda *_: (0,) * len(shape))


TABLE = (2, HALF, N)


def z_forward(density, table):
    return pl.pallas_call(
        head_kernel,
        grid=(2,),
        in_specs=[pl.BlockSpec((2, 8, 64, N), lambda i: (0, i, 0, 0)), whole(TABLE)],
        out_specs=pl.BlockSpec((128, 4, 8, 128), lambda i: (0, 0, i, 0)),
        out_shape=jax.ShapeDtypeStruct((128, 4, 16, 128), F32),
        compiler_params=pltpu.CompilerParams(vmem_limit_bytes=56 * MIB),
    )(density.reshape(2, 16, 64, N), table)


def filter_planes(planes, weights, table, back):
    return pl.pallas_call(
        middle_kernel,
        grid=(4,),
        in_specs=[
            pl.BlockSpec((GX, GY, 1, 16, 128), lambda s: (0, 0, s, 0, 0)),
            pl.BlockSpec((1, 2, HALF + 8, HALF + QUARTER), lambda s: (jnp.minimum(s, 2), 0, 0, 0)),
            pl.BlockSpec(memory_space=pltpu.VMEM),
            pl.BlockSpec(memory_space=pltpu.VMEM),
        ],
        out_specs=pl.BlockSpec((GX, GY, 1, 2, 16, 128), lambda s: (0, 0, s, 0, 0, 0)),
        out_shape=jax.ShapeDtypeStruct((GX, GY, 4, 2, 16, 128), F32),
        scratch_shapes=[
            *[pltpu.VMEM((GX, 2, 16, N), BF16) for _ in range(6)],
            *[pltpu.VMEM((N, HALF), BF16) for _ in range(12)],
        ],
        compiler_params=pltpu.CompilerParams(vmem_limit_bytes=28 * MIB),
    )(planes, weights, table, back)


def z_inverse(filtered, table):
    out = pl.pallas_call(
        tail_kernel,
        in_specs=[pl.BlockSpec(memory_space=pltpu.VMEM), pl.BlockSpec(memory_space=pltpu.VMEM)],
        out_specs=pl.BlockSpec(memory_space=pl.ANY),
        out_shape=jax.ShapeDtypeStruct((2, 2, 16, 64, N), F32),
        scratch_shapes=[
            pltpu.VMEM((4, 8, 2, 64, N), F32),
            pltpu.SemaphoreType.DMA((32,)),
            *[pltpu.VMEM((1024, N), BF16) for _ in range(4)],
            *[pltpu.VMEM((8, 128, HALF), F32) for _ in range(2)],
        ],
        compiler_params=pltpu.CompilerParams(vmem_limit_bytes=28 * MIB),
    )(filtered, table)
    return out.reshape(2, 32, 64, N)


def exchange(pieces):
    return lax.all_to_all(pieces, AXES, split_axis=0, concat_axis=0, tiled=True)


def per_device(density, radius_cells):
    table = two_parts(basis())
    back = two_parts(basis().transpose(0, 2, 1))
    planes = exchange(z_forward(density, table))
    weights = plane_windows(radius_cells)
    filtered = filter_planes(planes.reshape(GX, GY, 4, 16, 128), weights, table, back)
    return z_inverse(exchange(filtered.reshape(128, 4, 2, 16, 128)), table)


def solution(mesh):
    return jax.shard_map(
        per_device,
        mesh=mesh,
        in_specs=(P("gx", "gy", None), P()),
        out_specs=P(None, "gx", "gy", None),
        check_vma=False,
    )
```
